32 devices in a mesh: groups: 2 (over x), seq: 16 (over z, y, core).
Axes of the slice: x: 2, y: 2, z: 4, core: 2. Of those that a mesh axis runs over, the one named last changes fastest.
Arguments:
- inputs: bfloat16 [16384, 768], P(('groups', 'seq')), parts along dimension 0, may hold values from -6 to 6
- gates: bfloat16 [16384, 768], P(('groups', 'seq')), parts along dimension 0, may hold values from -6 to 6
- cotangent: bfloat16 [16384, 768], P(('groups', 'seq')), parts along dimension 0, may hold values from -6 to 6
- first_factor: bfloat16 [16, 512, 512], P('seq'), may hold values from -0.25 to 0.25
- second_factor: bfloat16 [512, 16, 16], P('seq'), may hold values from -1.5 to 1.5
- channel_gain: float32 [768], replicated, may hold values from 0.1 to 1.9
Outputs:
- layer_output: bfloat16 [16384, 768], P(('groups', 'seq')), parts along dimension 0
- grad_inputs: bfloat16 [16384, 768], P(('groups', 'seq')), parts along dimension 0
- grad_gates: bfloat16 [16384, 768], P(('groups', 'seq')), parts along dimension 0
- grad_first: bfloat16 [32, 512, 512], P(('groups', 'seq')), parts along dimension 0
- grad_second: bfloat16 [1024, 16, 16], P(('groups', 'seq')), parts along dimension 0
- gain_grad: float32 [1536], P('groups'), parts along dimension 0
The draws below stay inside these ranges and needn't reach their ends.
There are 2 independent parts, one for each index of `groups`. The reference program is written for one: setup_inputs(seed, part) draws one part's arguments, and reference() takes and returns one part's arrays. A program takes and returns all parts, laid end to end along the dimension named above; an argument that names none is the same for every part. Nothing has to cross between parts.
All inputs are finite; a program needn't handle non-finite values.
Results may differ from the reference program's by a relative error of at most 0.0085.
Values may be sent and summed in bfloat16 or wider, within the bound.
A program may use at most 64 MiB of HBM per device.

```python
import jax
import jax.numpy as jnp
from jax import lax

D = 768
BLOCK = 512
NBLOCKS = 16
TOKENS = 8192


def shard_levels(key, shape, shards, least, high):
    level, own = 1.0, jax.random.fold_in(key, 6)
    for dim, blocks in shards:
        steps = jnp.exp(jax.random.uniform(jax.random.fold_in(own, dim), (blocks,), jnp.float32, least / len(shards), high / len(shards)))
        level = level * jnp.repeat(steps, shape[dim] // blocks).reshape([-1 if axis == dim else 1 for axis in range(len(shape))])
    return level


def normal_values(own_key, shape, width, reach, shards=(), kind=jnp.bfloat16):
    values = width * jax.random.normal(own_key, shape, jnp.float32)
    if shards:
        values = values * shard_levels(own_key, shape, shards, -0.22, 0.18)
    return jnp.clip(values, -reach, reach).astype(kind)


def setup_inputs(seed: int = 0, part: int = 0) -> dict:
    seeds = jax.random.split(jax.random.key(seed), 7)
    own_keys = jax.random.split(jax.random.fold_in(seeds[6], part), 7)
    inputs = normal_values(own_keys[0], (TOKENS, D), 1.0, 6.0, ((0, 16),))
    gates = normal_values(own_keys[1], (TOKENS, D), 1.0, 6.0, ((0, 16),))
    cotangent = normal_values(own_keys[2], (TOKENS, D), 1.0, 6.0, ((0, 16),))
    first_factor = normal_values(seeds[3], (NBLOCKS, BLOCK, BLOCK), BLOCK ** -0.5, 0.25, ((0, 16),))
    second_factor = normal_values(seeds[4], (BLOCK, NBLOCKS, NBLOCKS), NBLOCKS ** -0.5, 1.5, ((0, 16),))
    channel_gain = jnp.clip(1.0 + 0.18 * jax.random.normal(seeds[5], (D,), jnp.float32), 0.1, 1.9)
    return dict(inputs=inputs, gates=gates, cotangent=cotangent, first_factor=first_factor, second_factor=second_factor, channel_gain=channel_gain)


def lower_mask(extent):
    row_ids = lax.broadcasted_iota(jnp.int32, (extent, extent), 0)
    col_ids = lax.broadcasted_iota(jnp.int32, (extent, extent), 1)
    return col_ids <= row_ids


def reference(inputs, gates, cotangent, first_factor, second_factor, channel_gain):
    rows3 = inputs.reshape(NBLOCKS, BLOCK, D)
    mask_first = lower_mask(BLOCK)
    mask_second = lower_mask(NBLOCKS)
    first_masked = jnp.where(mask_first[None], first_factor, jnp.zeros((), first_factor.dtype))
    second_masked = jnp.where(mask_second[None], second_factor, jnp.zeros((), second_factor.dtype))
    first_mixed = lax.map(lambda pair: jnp.dot(pair[0], pair[1], preferred_element_type=jnp.float32).astype(jnp.bfloat16), (first_masked, rows3))
    first_cols = jnp.swapaxes(first_mixed, 0, 1)
    second_cols = lax.map(lambda pair: jnp.dot(pair[0], pair[1], preferred_element_type=jnp.float32).astype(jnp.bfloat16), (second_masked, first_cols))
    second_mixed = jnp.swapaxes(second_cols, 0, 1).astype(jnp.float32)
    gates3 = gates.reshape(NBLOCKS, BLOCK, D).astype(jnp.float32)
    upstream = cotangent.reshape(NBLOCKS, BLOCK, D).astype(jnp.float32)
    layer_output = (gates3 * channel_gain * second_mixed).astype(jnp.bfloat16)
    grad_hidden = (upstream * gates3 * channel_gain).astype(jnp.bfloat16)
    grad_gates = (upstream * channel_gain * second_mixed).astype(jnp.bfloat16)
    gain_grad = jnp.sum(upstream * gates3 * second_mixed, axis=(0, 1)) * (1.0 / (TOKENS ** 0.5))
    hidden_cols = jnp.swapaxes(grad_hidden, 0, 1)
    grad_second = lax.map(lambda pair: jnp.where(mask_second, jnp.dot(pair[0], pair[1].T, preferred_element_type=jnp.float32), jnp.zeros((), jnp.float32)).astype(jnp.bfloat16), (hidden_cols, first_cols))
    back_cols = lax.map(lambda pair: jnp.dot(pair[0].T, pair[1], preferred_element_type=jnp.float32).astype(jnp.bfloat16), (second_masked, hidden_cols))
    back_rows = jnp.swapaxes(back_cols, 0, 1)
    grad_first = lax.map(lambda pair: jnp.where(mask_first, jnp.dot(pair[0], pair[1].T, preferred_element_type=jnp.float32), jnp.zeros((), jnp.float32)).astype(jnp.bfloat16), (back_rows, rows3))
    grad_inputs = lax.map(lambda pair: jnp.dot(pair[0].T, pair[1], preferred_element_type=jnp.float32).astype(jnp.bfloat16), (first_masked, back_rows))
    return (layer_output.reshape(TOKENS, D), grad_inputs.reshape(TOKENS, D), grad_gates.reshape(TOKENS, D), grad_first, grad_second, gain_grad)
```

```python
import functools
import math

import jax
import jax.numpy as jnp
from jax import lax
from jax.experimental import pallas as pl
from jax.experimental.pallas import tpu as pltpu
from jax.sharding import PartitionSpec as P

BF16 = jnp.bfloat16
F32 = jnp.float32


def lower_mask(extent):
    row_ids = lax.broadcasted_iota(jnp.int32, (extent, extent), 0)
    col_ids = lax.broadcasted_iota(jnp.int32, (extent, extent), 1)
    return col_ids <= row_ids


def dot(a, b, ca=1, cb=0):
    return lax.dot_general(a, b, (((ca,), (cb,)), ((), ())), preferred_element_type=F32)


def fused_kernel(
    n, x_ref, g_ref, u_ref, f_ref, s_ref, gain_ref,
    out_ref, gin_ref, ggate_ref, gfirst_ref, gsec_ref, ggain_ref,
    f_masked, weights, gh_rows, fm_rows, gh_cols, fm_cols, back_cols, sec_cols, back_rows, sec_rows,
    gain_all, send, recv,
):
    block, channels = x_ref.shape
    jpd = block // n
    me = lax.axis_index("seq")
    barrier = pltpu.get_barrier_semaphore()

    @pl.loop(1, n)
    def _(k):
        pl.semaphore_signal(
            barrier, inc=1, device_id={"seq": lax.rem(me + k, n)}, device_id_type=pl.DeviceIdType.MESH
        )

    def copy_to(phase, src, dst, peer, src_slot):
        return pltpu.make_async_remote_copy(
            src_ref=src.at[src_slot],
            dst_ref=dst.at[me],
            send_sem=send.at[phase, peer],
            recv_sem=recv.at[phase, me],
            device_id={"seq": peer},
            device_id_type=pl.DeviceIdType.MESH,
        )

    def copy_from(phase, src, dst, peer, src_slot):
        return pltpu.make_async_remote_copy(
            src_ref=src.at[src_slot],
            dst_ref=dst.at[peer],
            send_sem=send.at[phase, peer],
            recv_sem=recv.at[phase, peer],
            device_id={"seq": peer},
            device_id_type=pl.DeviceIdType.MESH,
        )

    def start_all(phase, src, dst):
        @pl.loop(1, n)
        def _(k):
            peer = lax.rem(me + k, n)
            copy_to(phase, src, dst, peer, peer).start()

    def wait_all(phase, src, dst):
        @pl.loop(1, n)
        def _(k):
            peer = lax.rem(me + k, n)
            copy_from(phase, src, dst, peer, peer).wait_recv()

    gain = gain_ref[...]
    rows = lambda ref: ref[...].reshape(block, channels)
    split = lambda value: value.reshape(n, jpd, channels)

    gh_rows[...] = split((u_ref[...].astype(F32) * g_ref[...].astype(F32) * gain).astype(BF16))
    pl.semaphore_wait(barrier, n - 1)
    start_all(0, gh_rows, gh_cols)
    gh_cols[me] = gh_rows[me]

    mask = lower_mask(block)
    f_masked[...] = jnp.where(mask, f_ref[...].astype(F32), 0.0).astype(BF16)
    fm_rows[...] = split(dot(f_masked[...], x_ref[...]).astype(BF16))
    start_all(1, fm_rows, fm_cols)
    fm_cols[me] = fm_rows[me]

    nb = s_ref.shape[1]
    s_rows = lax.broadcasted_iota(jnp.int32, (block, nb), 0)
    s_lanes = lax.broadcasted_iota(jnp.int32, (block, nb), 1)
    causal = s_lanes <= s_rows // jpd
    place = (
        lax.broadcasted_iota(jnp.int32, (nb, block), 0)
        == lax.broadcasted_iota(jnp.int32, (nb, block), 1) // jpd
    )
    place = jnp.where(place, 1.0, 0.0).astype(BF16)
    same = (
        lax.broadcasted_iota(jnp.int32, (block, block), 0) % jpd
        == lax.broadcasted_iota(jnp.int32, (block, block), 1) % jpd
    )
    s_masked = jnp.where(causal, s_ref[...].astype(F32), 0.0).astype(BF16)
    weights[...] = jnp.where(same, dot(s_masked, place), 0.0).astype(BF16)

    wait_all(0, gh_rows, gh_cols)
    back_cols[...] = split(dot(weights[...], rows(gh_cols), 0, 0).astype(BF16))
    start_all(2, back_cols, back_rows)
    back_rows[me] = back_cols[me]

    wait_all(1, fm_rows, fm_cols)
    second = dot(weights[...], rows(fm_cols)).astype(BF16)
    sec_cols[...] = split(second)
    start_all(3, sec_cols, sec_rows)
    sec_rows[me] = sec_cols[me]

    products = rows(gh_cols).astype(F32) * second.astype(F32)
    gain_all[me] = jnp.sum(products.reshape(block // 8, 8, channels), axis=0)

    @pl.loop(1, n)
    def _(k):
        peer = lax.rem(me + k, n)
        copy_to(4, gain_all, gain_all, peer, me).start()

    pairs = jnp.where(same, dot(rows(gh_cols), rows(fm_cols), 1, 1), 0.0).astype(BF16)
    gsec_ref[...] = jnp.where(causal, dot(pairs, place, 1, 1), 0.0).astype(BF16)

    wait_all(2, back_cols, back_rows)
    back = rows(back_rows)
    gfirst_ref[...] = jnp.where(mask, dot(back, x_ref[...], 1, 1), 0.0).astype(BF16)
    gin_ref[...] = dot(f_masked[...], back, 0, 0).astype(BF16)

    wait_all(3, sec_cols, sec_rows)
    hidden = rows(sec_rows).astype(F32) * gain
    out_ref[...] = (g_ref[...].astype(F32) * hidden).astype(BF16)
    ggate_ref[...] = (u_ref[...].astype(F32) * hidden).astype(BF16)

    @pl.loop(1, n)
    def _(k):
        peer = lax.rem(me + k, n)
        copy_from(4, gain_all, gain_all, peer, me).wait_recv()

    total = jnp.sum(jnp.sum(gain_all[...], axis=0), axis=0, keepdims=True)
    ggain_ref[...] = total / gain * (1.0 / math.sqrt(block * n))

    @pl.loop(1, n)
    def _(k):
        peer = lax.rem(me + k, n)
        copy_to(0, gh_rows, gh_cols, peer, peer).wait_send()
        copy_to(1, fm_rows, fm_cols, peer, peer).wait_send()
        copy_to(2, back_cols, back_rows, peer, peer).wait_send()
        copy_to(3, sec_cols, sec_rows, peer, peer).wait_send()
        copy_to(4, gain_all, gain_all, peer, me).wait_send()


def fused(n, inputs, gates, cotangent, first_factor, second_factor, channel_gain):
    block, channels = inputs.shape
    jpd, nb = second_factor.shape[0], second_factor.shape[1]
    s_rows = jnp.swapaxes(second_factor, 0, 1).reshape(nb * jpd, nb)
    tokens = jax.ShapeDtypeStruct((block, channels), BF16)
    exchange = pltpu.VMEM((n, jpd, channels), BF16)
    out, gin, ggate, gfirst, gsec, ggain = pl.pallas_call(
        functools.partial(fused_kernel, n),
        out_shape=(
            tokens, tokens, tokens,
            jax.ShapeDtypeStruct((block, block), BF16),
            jax.ShapeDtypeStruct((nb * jpd, nb), BF16),
            jax.ShapeDtypeStruct((1, channels), F32),
        ),
        in_specs=[pl.BlockSpec(memory_space=pltpu.VMEM)] * 6,
        out_specs=[pl.BlockSpec(memory_space=pltpu.VMEM)] * 6,
        scratch_shapes=[
            pltpu.VMEM((block, block), BF16),
            pltpu.VMEM((block, block), BF16),
            *[exchange] * 8,
            pltpu.VMEM((n, 8, channels), F32),
            pltpu.SemaphoreType.DMA((5, n)),
            pltpu.SemaphoreType.DMA((5, n)),
        ],
        compiler_params=pltpu.CompilerParams(
            collective_id=0, has_side_effects=True, vmem_limit_bytes=48 * 1024 * 1024
        ),
    )(inputs, gates, cotangent, first_factor[0], s_rows, channel_gain[None])
    gsec = jnp.swapaxes(gsec.reshape(nb, jpd, nb), 0, 1)
    return out, gin, ggate, gfirst[None], gsec, ggain[0]


def exchanged(inputs, gates, cotangent, first_factor, second_factor, channel_gain):
    block_count, block_size = first_factor.shape[:2]
    token_rows, channels = inputs.shape
    mask_first = lower_mask(block_size)
    mask_second = lower_mask(second_factor.shape[1])
    first_masked = jnp.where(mask_first[None], first_factor, jnp.zeros((), BF16))
    second_masked = jnp.where(mask_second[None], second_factor, jnp.zeros((), BF16))
    norm_factor = 1.0 / math.sqrt(token_rows * lax.axis_size("seq"))
    by_block = lambda value: value.reshape(block_count, block_size, channels)
    rows3 = by_block(inputs)
    gates3 = by_block(gates).astype(F32)
    upstream3 = by_block(cotangent).astype(F32)
    to_cols = lambda value: lax.all_to_all(value, "seq", split_axis=1, concat_axis=0, tiled=True)
    to_rows = lambda value: lax.all_to_all(value, "seq", split_axis=0, concat_axis=1, tiled=True)
    product = functools.partial(jnp.einsum, preferred_element_type=F32)
    hidden_cols = to_cols((upstream3 * gates3 * channel_gain).astype(BF16))
    columns = to_cols(product("kab,kbc->kac", first_masked, rows3).astype(BF16))
    back_rows = to_rows(product("jab,ajc->bjc", second_masked, hidden_cols).astype(BF16))
    second_rows = to_rows(product("jab,bjc->ajc", second_masked, columns).astype(BF16)).astype(F32)
    pairs = product("ajc,bjc->jab", hidden_cols, columns)
    grad_sec = jnp.where(mask_second[None], pairs, 0.0).astype(BF16)
    pairs_first = product("kac,kbc->kab", back_rows, rows3)
    grad_first = jnp.where(mask_first[None], pairs_first, 0.0).astype(BF16)
    grad_in = product("kab,kac->kbc", first_masked, back_rows).astype(BF16)
    out = (gates3 * channel_gain * second_rows).astype(BF16)
    grad_gate = (upstream3 * channel_gain * second_rows).astype(BF16)
    gain_grad = lax.psum(jnp.sum(upstream3 * gates3 * second_rows, axis=(0, 1)), "seq") * norm_factor
    flat = lambda value: value.reshape(token_rows, channels)
    return flat(out), flat(grad_in), flat(grad_gate), grad_first, grad_sec, gain_grad


def on_device(*args):
    n = lax.axis_size("seq")
    first_factor, second_factor = args[3], args[4]
    if first_factor.shape[0] == 1 and second_factor.shape[0] % 16 == 0:
        return fused(n, *args)
    return exchanged(*args)


def solution(mesh):
    placed = (
        P(("groups", "seq"), None),
        P(("groups", "seq"), None),
        P(("groups", "seq"), None),
        P("seq", None, None),
        P("seq", None, None),
        P(),
    )
    return jax.shard_map(
        on_device,
        mesh=mesh,
        in_specs=placed,
        out_specs=(
            P(("groups", "seq"), None),
            P(("groups", "seq"), None),
            P(("groups", "seq"), None),
            P(("groups", "seq"), None, None),
            P(("groups", "seq"), None, None),
            P("groups"),
        ),
        check_vma=False,
    )
```

```python
import functools
import math

import jax
import jax.numpy as jnp
from jax import lax
from jax.experimental import pallas as pl
from jax.experimental.pallas import tpu as pltpu
from jax.sharding import PartitionSpec as P

BF16 = jnp.bfloat16
F32 = jnp.float32


def lower_mask(extent):
    row_ids = lax.broadcasted_iota(jnp.int32, (extent, extent), 0)
    col_ids = lax.broadcasted_iota(jnp.int32, (extent, extent), 1)
    return col_ids <= row_ids


def dot(a, b, ca=1, cb=0):
    return lax.dot_general(a, b, (((ca,), (cb,)), ((), ())), preferred_element_type=F32)


def fused_kernel(
    n, x_ref, g_ref, u_ref, f_ref, s_ref, gain_ref,
    out_ref, gin_ref, ggate_ref, gfirst_ref, gsec_ref, ggain_ref,
    f_masked, weights, s_all, gh_rows, fm_rows, gh_cols, fm_cols, back_cols, sec_cols, back_rows, sec_rows,
    part_out, part_in, gsec_part, gsec_in, gain_all,
    flat_send, flat_recv, line_send, line_recv, part_send, part_recv, small_send, small_recv, gain_send, gain_recv,
):
    block, channels = x_ref.shape
    jpd = block // n
    side = 4
    tile = side * jpd
    me = lax.axis_index("seq")
    z, q = me // side, lax.rem(me, side)
    barrier = pltpu.get_barrier_semaphore()

    @pl.loop(1, n)
    def _(k):
        pl.semaphore_signal(
            barrier, inc=1, device_id={"seq": lax.rem(me + k, n)}, device_id_type=pl.DeviceIdType.MESH
        )

    def remote(src, dst, send, recv, peer):
        return pltpu.make_async_remote_copy(
            src_ref=src, dst_ref=dst, send_sem=send, recv_sem=recv,
            device_id={"seq": peer}, device_id_type=pl.DeviceIdType.MESH,
        )

    def flat_pair(phase, t, peer_q, slot):
        if phase == 0:
            return gh_rows.at[t, peer_q], gh_cols.at[t, z, slot]
        if phase == 1:
            return fm_rows.at[t, peer_q], fm_cols.at[t, z, slot]
        if phase == 2:
            return back_cols.at[t, peer_q], back_rows.at[t, slot]
        return sec_cols.at[t, peer_q], sec_rows.at[t, slot]

    def flat_copy(phase, t, peer_q, slot):
        src, dst = flat_pair(phase, t, peer_q, slot)
        return remote(
            src, dst, flat_send.at[phase, t, peer_q], flat_recv.at[phase, t, slot], z * side + peer_q
        )

    def flat_start(phase, t):
        @pl.loop(1, side)
        def _(k):
            peer_q = lax.rem(q + k, side)
            flat_copy(phase, t, peer_q, q).start()

    def flat_wait(phase, t):
        @pl.loop(1, side)
        def _(k):
            peer_q = lax.rem(q + k, side)
            flat_copy(phase, t, peer_q, peer_q).wait_recv()

    def line_copy(phase, t, source, target):
        cols = gh_cols if phase == 0 else fm_cols
        return remote(
            cols.at[t, source], cols.at[t, source],
            line_send.at[phase, t, target], line_recv.at[phase, t, source], target * side + q,
        )

    line_routes = {0: ((1, 0, 1), (1, 0, 2)), 1: ((1, 1, 2),), 2: ((0, 2, 1),), 3: ((0, 3, 2), (0, 3, 1))}

    def part_copy(t, target):
        return remote(part_out.at[t], part_in.at[t], part_send.at[t], part_recv.at[t], target * side + q)

    def s_copy(target, source):
        return remote(
            s_all.at[z], s_all.at[source], small_send.at[0, target], small_recv.at[0, source], target * side + q
        )

    def gsec_copy(target, source):
        return remote(
            gsec_part.at[target], gsec_in.at[source],
            small_send.at[1, target], small_recv.at[1, source], target * side + q,
        )

    def gain_copy(peer, source):
        return remote(gain_all.at[me], gain_all.at[source], gain_send.at[peer], gain_recv.at[source], peer)

    gain = gain_ref[...]
    by_piece = lambda value: value.reshape(side, side, jpd, channels)
    piece = lambda value: value.astype(BF16).reshape(side, jpd, channels)
    flat = lambda value: value.reshape(-1, channels)

    gh_rows[...] = by_piece((u_ref[...].astype(F32) * g_ref[...].astype(F32) * gain).astype(BF16))
    nb = s_ref.shape[0]
    up = lax.broadcasted_iota(jnp.int32, (nb, block), 0)
    causal = up <= lax.broadcasted_iota(jnp.int32, (nb, block), 1) // jpd
    s_all[z] = jnp.where(causal, s_ref[...].astype(F32), 0.0).astype(BF16)
    gsec_part[...] = jnp.zeros_like(gsec_part)

    pl.semaphore_wait(barrier, n - 1)
    flat_start(0, 0)

    @pl.loop(1, side)
    def _(k):
        target = lax.rem(z + k, side)
        s_copy(target, z).start()

    mask = lower_mask(block)
    f_masked[...] = jnp.where(mask, f_ref[...].astype(F32), 0.0).astype(BF16)
    fm_rows[...] = by_piece(dot(f_masked[...], x_ref[...]).astype(BF16))
    for t in range(side):
        flat_start(1, t)
        if t + 1 < side:
            flat_start(0, t + 1)
    for t in range(side):
        gh_cols[t, z, q] = gh_rows[t, q]
        fm_cols[t, z, q] = fm_rows[t, q]

    @pl.loop(1, side)
    def _(k):
        source = lax.rem(z + k, side)
        s_copy(source, source).wait_recv()

    place = (
        lax.broadcasted_iota(jnp.int32, (block, nb), 0) // jpd
        == lax.broadcasted_iota(jnp.int32, (block, nb), 1)
    )
    place = jnp.where(place, 1.0, 0.0).astype(BF16)
    same = (
        lax.broadcasted_iota(jnp.int32, (block, block), 0) % jpd
        == lax.broadcasted_iota(jnp.int32, (block, block), 1) % jpd
    )

    @pl.loop(0, side)
    def _(t):
        flat_wait(0, t)
        flat_wait(1, t)
        for role, routes in line_routes.items():
            @pl.when(z == role)
            def _():
                for phase, source, target in routes:
                    line_copy(phase, t, source, target).start()
        weights[t] = jnp.where(same, dot(place, s_all[t]), 0.0).astype(BF16)

    def add_pairs(t, low, high, first, last):
        rows, lanes = (high - low) * tile, (last - first) * tile
        own = (
            lax.broadcasted_iota(jnp.int32, (rows, lanes), 0) % jpd
            == lax.broadcasted_iota(jnp.int32, (rows, lanes), 1) % jpd
        )
        pairs = dot(flat(fm_cols[t, low:high]), flat(gh_cols[t, first:last]), 1, 1)
        pairs = jnp.where(own, pairs, 0.0).astype(BF16)
        sums = dot(place[low * tile:high * tile], pairs, 0, 0).astype(BF16)
        gsec_part[t, :, first * tile:last * tile] = gsec_part[t, :, first * tile:last * tile] + sums

    def send_second(t, second, plane):
        sec_cols[t] = piece(second)
        flat_start(3, t)
        products = second.astype(BF16).astype(F32) * flat(gh_cols[t, plane]).astype(F32)
        sums = jnp.sum(products.reshape(tile // 8, 8, channels), axis=0)
        gain_all[me] = jnp.where(t == 0, 0.0, gain_all[me]) + sums

    def send_back(t, back):
        back_cols[t] = piece(back)
        flat_start(2, t)

    w = lambda t, low, high, first, last: weights[t, low * tile:high * tile, first * tile:last * tile]

    gain_all[me] = jnp.zeros((8, channels), F32)

    @pl.when(z == 0)
    def _():
        @pl.loop(0, side)
        def _(t):
            send_second(t, dot(w(t, 0, 1, 0, 1), flat(fm_cols[t, 0:1]), 0, 0), 0)
            add_pairs(t, 0, 1, 0, 1)

        @pl.loop(0, side)
        def _(t):
            back = dot(w(t, 0, 1, 0, 1), flat(gh_cols[t, 0:1]))
            part_copy(t, 0).wait_recv()
            send_back(t, back + flat(part_in[t]).astype(F32))

    @pl.when(z == 3)
    def _():
        @pl.loop(0, side)
        def _(t):
            send_back(t, dot(w(t, 3, 4, 3, 4), flat(gh_cols[t, 3:4])))
            add_pairs(t, 3, 4, 3, 4)

        @pl.loop(0, side)
        def _(t):
            second = dot(w(t, 3, 4, 3, 4), flat(fm_cols[t, 3:4]), 0, 0)
            part_copy(t, 3).wait_recv()
            send_second(t, second + flat(part_in[t]).astype(F32), 3)

    @pl.when(z == 1)
    def _():
        @pl.loop(0, side)
        def _(t):
            line_copy(0, t, 2, 1).wait_recv()
            line_copy(0, t, 3, 1).wait_recv()
            both = dot(w(t, 0, 2, 1, 4), flat(gh_cols[t, 1:4]))
            part_out[t] = piece(both[:tile])
            part_copy(t, 0).start()
            send_back(t, both[tile:])
            line_copy(1, t, 0, 1).wait_recv()
            send_second(t, dot(w(t, 0, 2, 1, 2), flat(fm_cols[t, 0:2]), 0, 0), 1)
            add_pairs(t, 0, 2, 1, 3)

    @pl.when(z == 2)
    def _():
        @pl.loop(0, side)
        def _(t):
            line_copy(1, t, 0, 2).wait_recv()
            line_copy(1, t, 1, 2).wait_recv()
            both = dot(w(t, 0, 3, 2, 4), flat(fm_cols[t, 0:3]), 0, 0)
            part_out[t] = piece(both[tile:])
            part_copy(t, 3).start()
            send_second(t, both[:tile], 2)
            line_copy(0, t, 3, 2).wait_recv()
            send_back(t, dot(w(t, 2, 3, 2, 4), flat(gh_cols[t, 2:4])))
            add_pairs(t, 0, 3, 3, 4)
            add_pairs(t, 2, 3, 2, 3)

    @pl.loop(1, n)
    def _(k):
        gain_copy(lax.rem(me + k, n), me).start()

    @pl.loop(1, side)
    def _(k):
        gsec_copy(lax.rem(z + k, side), z).start()

    for t in range(side):
        back_rows[t, q] = back_cols[t, q]
        sec_rows[t, q] = sec_cols[t, q]
    for t in range(side):
        rows = slice(t * tile, (t + 1) * tile)
        flat_wait(3, t)
        hidden = flat(sec_rows[t]).astype(F32) * gain
        out_ref[rows] = (g_ref[rows].astype(F32) * hidden).astype(BF16)
        ggate_ref[rows] = (u_ref[rows].astype(F32) * hidden).astype(BF16)
        flat_wait(2, t)
        first = dot(flat(back_rows[t]), x_ref[...], 1, 1)
        gfirst_ref[rows] = jnp.where(mask[rows], first, 0.0).astype(BF16)
    gin_ref[...] = dot(f_masked[...], flat(back_rows[...]), 0, 0).astype(BF16)

    gsec_in[z] = gsec_part[z]

    @pl.loop(1, side)
    def _(k):
        source = lax.rem(z + k, side)
        gsec_copy(source, source).wait_recv()

    gsec_sum = jnp.sum(gsec_in[...].astype(F32), axis=0)
    gsec_ref[...] = jnp.where(causal, gsec_sum, 0.0).astype(BF16)

    @pl.loop(1, n)
    def _(k):
        peer = lax.rem(me + k, n)
        gain_copy(peer, peer).wait_recv()

    total = jnp.sum(jnp.sum(gain_all[...], axis=0), axis=0, keepdims=True)
    ggain_ref[...] = total / gain * (1.0 / math.sqrt(block * n))

    @pl.loop(0, side)
    def _(t):
        @pl.loop(1, side)
        def _(k):
            peer_q = lax.rem(q + k, side)
            for phase in range(4):
                flat_copy(phase, t, peer_q, q).wait_send()
        for role, routes in line_routes.items():
            @pl.when(z == role)
            def _():
                for phase, source, target in routes:
                    line_copy(phase, t, source, target).wait_send()
                if role in (1, 2):
                    part_copy(t, 0 if role == 1 else 3).wait_send()

    @pl.loop(1, side)
    def _(k):
        target = lax.rem(z + k, side)
        s_copy(target, z).wait_send()
        gsec_copy(target, z).wait_send()

    @pl.loop(1, n)
    def _(k):
        gain_copy(lax.rem(me + k, n), me).wait_send()


def fused(n, inputs, gates, cotangent, first_factor, second_factor, channel_gain):
    block, channels = inputs.shape
    jpd, nb = second_factor.shape[0], second_factor.shape[1]
    side = 4
    s_lanes = jnp.transpose(second_factor, (2, 1, 0)).reshape(nb, nb * jpd)
    tokens = jax.ShapeDtypeStruct((block, channels), BF16)
    pieces = pltpu.VMEM((side, side, jpd, channels), BF16)
    planes = pltpu.VMEM((side, side, side, jpd, channels), BF16)
    small = pltpu.VMEM((side, nb, block), BF16)
    dma = pltpu.SemaphoreType.DMA
    out, gin, ggate, gfirst, gsec, ggain = pl.pallas_call(
        functools.partial(fused_kernel, n),
        out_shape=(
            tokens, tokens, tokens,
            jax.ShapeDtypeStruct((block, block), BF16),
            jax.ShapeDtypeStruct((nb, block), BF16),
            jax.ShapeDtypeStruct((1, channels), F32),
        ),
        in_specs=[pl.BlockSpec(memory_space=pltpu.VMEM)] * 6,
        out_specs=[pl.BlockSpec(memory_space=pltpu.VMEM)] * 6,
        scratch_shapes=[
            pltpu.VMEM((block, block), BF16),
            pltpu.VMEM((side, block, block), BF16),
            small,
            pieces, pieces, planes, planes, pieces, pieces, pieces, pieces, pieces, pieces,
            small, small,
            pltpu.VMEM((n, 8, channels), F32),
            dma((4, side, side)), dma((4, side, side)),
            dma((2, side, side)), dma((2, side, side)),
            dma((side,)), dma((side,)),
            dma((2, side)), dma((2, side)),
            dma((n,)), dma((n,)),
        ],
        compiler_params=pltpu.CompilerParams(
            collective_id=0, has_side_effects=True, vmem_limit_bytes=48 * 1024 * 1024
        ),
    )(inputs, gates, cotangent, first_factor[0], s_lanes, channel_gain[None])
    gsec = jnp.transpose(gsec.reshape(nb, nb, jpd), (2, 1, 0))
    return out, gin, ggate, gfirst[None], gsec, ggain[0]


def exchanged(inputs, gates, cotangent, first_factor, second_factor, channel_gain):
    block_count, block_size = first_factor.shape[:2]
    token_rows, channels = inputs.shape
    mask_first = lower_mask(block_size)
    mask_second = lower_mask(second_factor.shape[1])
    first_masked = jnp.where(mask_first[None], first_factor, jnp.zeros((), BF16))
    second_masked = jnp.where(mask_second[None], second_factor, jnp.zeros((), BF16))
    norm_factor = 1.0 / math.sqrt(token_rows * lax.axis_size("seq"))
    by_block = lambda value: value.reshape(block_count, block_size, channels)
    rows3 = by_block(inputs)
    gates3 = by_block(gates).astype(F32)
    upstream3 = by_block(cotangent).astype(F32)
    to_cols = lambda value: lax.all_to_all(value, "seq", split_axis=1, concat_axis=0, tiled=True)
    to_rows = lambda value: lax.all_to_all(value, "seq", split_axis=0, concat_axis=1, tiled=True)
    product = functools.partial(jnp.einsum, preferred_element_type=F32)
    hidden_cols = to_cols((upstream3 * gates3 * channel_gain).astype(BF16))
    columns = to_cols(product("kab,kbc->kac", first_masked, rows3).astype(BF16))
    back_rows = to_rows(product("jab,ajc->bjc", second_masked, hidden_cols).astype(BF16))
    second_rows = to_rows(product("jab,bjc->ajc", second_masked, columns).astype(BF16)).astype(F32)
    pairs = product("ajc,bjc->jab", hidden_cols, columns)
    grad_sec = jnp.where(mask_second[None], pairs, 0.0).astype(BF16)
    pairs_first = product("kac,kbc->kab", back_rows, rows3)
    grad_first = jnp.where(mask_first[None], pairs_first, 0.0).astype(BF16)
    grad_in = product("kab,kac->kbc", first_masked, back_rows).astype(BF16)
    out = (gates3 * channel_gain * second_rows).astype(BF16)
    grad_gate = (upstream3 * channel_gain * second_rows).astype(BF16)
    gain_grad = lax.psum(jnp.sum(upstream3 * gates3 * second_rows, axis=(0, 1)), "seq") * norm_factor
    flat = lambda value: value.reshape(token_rows, channels)
    return flat(out), flat(grad_in), flat(grad_gate), grad_first, grad_sec, gain_grad


def on_device(*args):
    n = lax.axis_size("seq")
    first_factor, second_factor = args[3], args[4]
    if n == 16 and first_factor.shape[0] == 1 and second_factor.shape[0] % 16 == 0:
        return fused(n, *args)
    return exchanged(*args)


def solution(mesh):
    placed = (
        P(("groups", "seq"), None),
        P(("groups", "seq"), None),
        P(("groups", "seq"), None),
        P("seq", None, None),
        P("seq", None, None),
        P(),
    )
    return jax.shard_map(
        on_device,
        mesh=mesh,
        in_specs=placed,
        out_specs=(
            P(("groups", "seq"), None),
            P(("groups", "seq"), None),
            P(("groups", "seq"), None),
            P(("groups", "seq"), None, None),
            P(("groups", "seq"), None, None),
            P("groups"),
        ),
        check_vma=False,
    )
```

```python
import functools
import math

import jax
import jax.numpy as jnp
from jax import lax
from jax.experimental import pallas as pl
from jax.experimental.pallas import tpu as pltpu
from jax.sharding import PartitionSpec as P

BF16 = jnp.bfloat16
F32 = jnp.float32


def lower_mask(extent):
    row_ids = lax.broadcasted_iota(jnp.int32, (extent, extent), 0)
    col_ids = lax.broadcasted_iota(jnp.int32, (extent, extent), 1)
    return col_ids <= row_ids


def dot(a, b, ca=1, cb=0):
    return lax.dot_general(a, b, (((ca,), (cb,)), ((), ())), preferred_element_type=F32)


def fused_kernel(
    n, x_hbm, g_hbm, u_hbm, f_hbm, s_ref, gain_ref,
    out_ref, gin_ref, ggate_ref, gfirst_ref, gsec_ref, ggain_ref,
    x_ref, g_ref, u_ref, f_ref, gin_acc, f_masked, weights, s_all, gh_rows, fm_rows, gh_cols, fm_cols, back_cols, sec_cols, back_rows, sec_rows,
    part_out, part_in, gsec_part, gsec_in, gain_part, gain_all,
    flat_send, flat_recv, line_send, line_recv, part_send, part_recv, small_send, small_recv, gain_send, gain_recv, load,
):
    block, channels = x_ref.shape
    jpd = block // n
    side = 4
    tile = side * jpd
    me = lax.axis_index("seq")
    z, q = me // side, lax.rem(me, side)
    loads = [
        pltpu.make_async_copy(src, dst, load.at[k])
        for k, (src, dst) in enumerate(((f_hbm, f_ref), (x_hbm, x_ref), (g_hbm, g_ref), (u_hbm, u_ref)))
    ]
    for copy in loads:
        copy.start()
    barrier = pltpu.get_barrier_semaphore()

    @pl.loop(1, n)
    def _(k):
        pl.semaphore_signal(
            barrier, inc=1, device_id={"seq": lax.rem(me + k, n)}, device_id_type=pl.DeviceIdType.MESH
        )

    def remote(src, dst, send, recv, peer):
        return pltpu.make_async_remote_copy(
            src_ref=src, dst_ref=dst, send_sem=send, recv_sem=recv,
            device_id={"seq": peer}, device_id_type=pl.DeviceIdType.MESH,
        )

    def flat_pair(phase, t, peer_q, slot):
        if phase == 0:
            return gh_rows.at[t, peer_q], gh_cols.at[t, z, slot]
        if phase == 1:
            return fm_rows.at[t, peer_q], fm_cols.at[t, z, slot]
        if phase == 2:
            return back_cols.at[t, peer_q], back_rows.at[t, slot]
        return sec_cols.at[t, peer_q], sec_rows.at[t, slot]

    def flat_copy(phase, t, peer_q, slot):
        src, dst = flat_pair(phase, t, peer_q, slot)
        return remote(
            src, dst, flat_send.at[phase, t, peer_q], flat_recv.at[phase, t, slot], z * side + peer_q
        )

    def flat_start(phase, t):
        @pl.loop(1, side)
        def _(k):
            peer_q = lax.rem(q + k, side)
            flat_copy(phase, t, peer_q, q).start()

    def flat_wait(phase, t):
        @pl.loop(1, side)
        def _(k):
            peer_q = lax.rem(q + k, side)
            flat_copy(phase, t, peer_q, peer_q).wait_recv()

    def line_copy(phase, t, source, target):
        cols = gh_cols if phase == 0 else fm_cols
        return remote(
            cols.at[t, source], cols.at[t, source],
            line_send.at[phase, t, target], line_recv.at[phase, t, source], target * side + q,
        )

    line_routes = {0: ((1, 0, 2), (1, 0, 1)), 1: ((1, 1, 2),), 2: ((0, 2, 1),), 3: ((0, 3, 1), (0, 3, 2))}

    def part_copy(t, target):
        return remote(part_out.at[t], part_in.at[t], part_send.at[t], part_recv.at[t], target * side + q)

    def s_copy(target, source):
        return remote(
            s_all.at[z], s_all.at[source], small_send.at[0, target], small_recv.at[0, source], target * side + q
        )

    def gsec_copy(target, source):
        return remote(
            gsec_part.at[target], gsec_in.at[source],
            small_send.at[1, target], small_recv.at[1, source], target * side + q,
        )

    def gain_copy(peer, source):
        return remote(gain_all.at[me], gain_all.at[source], gain_send.at[peer], gain_recv.at[source], peer)

    gain = gain_ref[...]
    by_piece = lambda value: value.reshape(side, side, jpd, channels)
    piece = lambda value: value.astype(BF16).reshape(side, jpd, channels)
    flat = lambda value: value.reshape(-1, channels)

    nb = s_ref.shape[0]
    up = lax.broadcasted_iota(jnp.int32, (nb, block), 0)
    causal = up <= lax.broadcasted_iota(jnp.int32, (nb, block), 1) // jpd
    s_all[z] = jnp.where(causal, s_ref[...].astype(F32), 0.0).astype(BF16)
    gsec_part[...] = jnp.zeros_like(gsec_part)

    for copy in loads:
        copy.wait()
    pl.semaphore_wait(barrier, n - 1)

    @pl.loop(1, side)
    def _(k):
        target = lax.rem(z + k, side)
        s_copy(target, z).start()

    def strip_mask(t):
        ids = lambda dim: lax.broadcasted_iota(jnp.int32, (tile, block), dim)
        return ids(1) <= ids(0) + t * tile

    def send_hidden():
        for t in range(side):
            rows = slice(t * tile, (t + 1) * tile)
            gh_rows[t] = piece(u_ref[rows].astype(F32) * g_ref[rows].astype(F32) * gain)
            flat_start(0, t)

    def send_mixed():
        for t in range(side):
            rows, depth = slice(t * tile, (t + 1) * tile), (t + 1) * tile
            f_masked[rows] = jnp.where(strip_mask(t), f_ref[rows].astype(F32), 0.0).astype(BF16)
            fm_rows[t] = piece(dot(f_masked[rows, :depth], x_ref[:depth]))
            flat_start(1, t)

    @pl.when(z < 2)
    def _():
        send_mixed()
        send_hidden()

    @pl.when(z >= 2)
    def _():
        send_hidden()
        send_mixed()

    for t in range(side):
        gh_cols[t, z, q] = gh_rows[t, q]
        fm_cols[t, z, q] = fm_rows[t, q]

    @pl.loop(1, side)
    def _(k):
        source = lax.rem(z + k, side)
        s_copy(source, source).wait_recv()

    place = (
        lax.broadcasted_iota(jnp.int32, (block, nb), 0) // jpd
        == lax.broadcasted_iota(jnp.int32, (block, nb), 1)
    )
    place = jnp.where(place, 1.0, 0.0).astype(BF16)
    same = (
        lax.broadcasted_iota(jnp.int32, (tile, block), 0) % jpd
        == lax.broadcasted_iota(jnp.int32, (tile, block), 1) % jpd
    )
    strips = {0: (0,), 1: (0, 1), 2: (0, 1, 2), 3: (3,)}

    @pl.loop(0, side)
    def _(t):
        for role, routes in line_routes.items():
            @pl.when(z == role)
            def _():
                for phase in ((1, 0) if role < 2 else (0, 1)):
                    if any(route[0] == phase for route in routes):
                        flat_wait(phase, t)
                for phase, source, target in routes:
                    line_copy(phase, t, source, target).start()
                for a in strips[role]:
                    rows = slice(a * tile, (a + 1) * tile)
                    weights[t, rows] = jnp.where(same, dot(place[rows], s_all[t]), 0.0).astype(BF16)

    def add_pairs(t, low, high, first, last):
        rows, lanes = (high - low) * tile, (last - first) * tile
        own = (
            lax.broadcasted_iota(jnp.int32, (rows, lanes), 0) % jpd
            == lax.broadcasted_iota(jnp.int32, (rows, lanes), 1) % jpd
        )
        pairs = dot(flat(fm_cols[t, low:high]), flat(gh_cols[t, first:last]), 1, 1)
        pairs = jnp.where(own, pairs, 0.0).astype(BF16)
        sums = dot(place[low * tile:high * tile], pairs, 0, 0).astype(BF16)
        gsec_part[t, :, first * tile:last * tile] = gsec_part[t, :, first * tile:last * tile] + sums

    def send_second(t, second, plane):
        sec_cols[t] = piece(second)
        flat_start(3, t)
        products = second.astype(BF16).astype(F32) * flat(gh_cols[t, plane]).astype(F32)
        gain_part[...] = gain_part[...] + jnp.sum(products.reshape(tile // 8, 8, channels), axis=0)

    def send_back(t, back):
        back_cols[t] = piece(back)
        flat_start(2, t)

    w = lambda t, low, high, first, last: weights[t, low * tile:high * tile, first * tile:last * tile]

    gain_part[...] = jnp.zeros_like(gain_part)

    @pl.when(z == 0)
    def _():
        @pl.loop(0, side)
        def _(t):
            flat_wait(0, t)
            send_second(t, dot(w(t, 0, 1, 0, 1), flat(fm_cols[t, 0:1]), 0, 0), 0)
            add_pairs(t, 0, 1, 0, 1)

        @pl.loop(0, side)
        def _(t):
            back = dot(w(t, 0, 1, 0, 1), flat(gh_cols[t, 0:1]))
            part_copy(t, 0).wait_recv()
            send_back(t, back + flat(part_in[t]).astype(F32))

    @pl.when(z == 3)
    def _():
        @pl.loop(0, side)
        def _(t):
            flat_wait(1, t)
            send_back(t, dot(w(t, 3, 4, 3, 4), flat(gh_cols[t, 3:4])))
            add_pairs(t, 3, 4, 3, 4)

        @pl.loop(0, side)
        def _(t):
            second = dot(w(t, 3, 4, 3, 4), flat(fm_cols[t, 3:4]), 0, 0)
            part_copy(t, 3).wait_recv()
            send_second(t, second + flat(part_in[t]).astype(F32), 3)

    @pl.when(z == 1)
    def _():
        @pl.loop(0, side)
        def _(t):
            flat_wait(0, t)
            line_copy(0, t, 2, 1).wait_recv()
            line_copy(0, t, 3, 1).wait_recv()
            both = dot(w(t, 0, 2, 1, 4), flat(gh_cols[t, 1:4]))
            part_out[t] = piece(both[:tile])
            part_copy(t, 0).start()
            send_back(t, both[tile:])
            line_copy(1, t, 0, 1).wait_recv()
            send_second(t, dot(w(t, 0, 2, 1, 2), flat(fm_cols[t, 0:2]), 0, 0), 1)
            add_pairs(t, 0, 2, 1, 3)

    @pl.when(z == 2)
    def _():
        @pl.loop(0, side)
        def _(t):
            flat_wait(1, t)
            line_copy(1, t, 0, 2).wait_recv()
            line_copy(1, t, 1, 2).wait_recv()
            both = dot(w(t, 0, 3, 2, 4), flat(fm_cols[t, 0:3]), 0, 0)
            part_out[t] = piece(both[tile:])
            part_copy(t, 3).start()
            send_second(t, both[:tile], 2)
            line_copy(0, t, 3, 2).wait_recv()
            send_back(t, dot(w(t, 2, 3, 2, 4), flat(gh_cols[t, 2:4])))
            add_pairs(t, 0, 3, 3, 4)
            add_pairs(t, 2, 3, 2, 3)

    gain_all[me] = jnp.sum(gain_part[...], axis=0, keepdims=True)

    @pl.loop(1, n)
    def _(k):
        gain_copy(lax.rem(me + k, n), me).start()

    @pl.loop(1, side)
    def _(k):
        gsec_copy(lax.rem(z + k, side), z).start()

    for t in range(side):
        back_rows[t, q] = back_cols[t, q]
        sec_rows[t, q] = sec_cols[t, q]
    last = block - tile
    for t in range(side):
        rows = slice(t * tile, (t + 1) * tile)
        flat_wait(3, t)
        hidden = flat(sec_rows[t]).astype(F32) * gain
        out_ref[rows] = (g_ref[rows].astype(F32) * hidden).astype(BF16)
        ggate_ref[rows] = (u_ref[rows].astype(F32) * hidden).astype(BF16)
        flat_wait(2, t)
        first = dot(flat(back_rows[t]), x_ref[...], 1, 1)
        gfirst_ref[rows] = jnp.where(strip_mask(t), first, 0.0).astype(BF16)
        if t == side - 2:
            gin_acc[:last] = dot(f_masked[:last, :last], flat(back_rows[:side - 1]), 0, 0)
    final = dot(f_masked[last:], flat(back_rows[side - 1]), 0, 0)
    gin_ref[:last] = (gin_acc[:last] + final[:last]).astype(BF16)
    gin_ref[last:] = final[last:].astype(BF16)

    gsec_in[z] = gsec_part[z]

    @pl.loop(1, side)
    def _(k):
        source = lax.rem(z + k, side)
        gsec_copy(source, source).wait_recv()

    gsec_sum = jnp.sum(gsec_in[...].astype(F32), axis=0)
    gsec_ref[...] = jnp.where(causal, gsec_sum, 0.0).astype(BF16)

    @pl.loop(1, n)
    def _(k):
        peer = lax.rem(me + k, n)
        gain_copy(peer, peer).wait_recv()

    total = jnp.sum(gain_all[...], axis=0)
    ggain_ref[...] = total / gain * (1.0 / math.sqrt(block * n))

    @pl.loop(0, side)
    def _(t):
        @pl.loop(1, side)
        def _(k):
            peer_q = lax.rem(q + k, side)
            for phase in range(4):
                flat_copy(phase, t, peer_q, q).wait_send()
        for role, routes in line_routes.items():
            @pl.when(z == role)
            def _():
                for phase, source, target in routes:
                    line_copy(phase, t, source, target).wait_send()
                if role in (1, 2):
                    part_copy(t, 0 if role == 1 else 3).wait_send()

    @pl.loop(1, side)
    def _(k):
        target = lax.rem(z + k, side)
        s_copy(target, z).wait_send()
        gsec_copy(target, z).wait_send()

    @pl.loop(1, n)
    def _(k):
        gain_copy(lax.rem(me + k, n), me).wait_send()


def fused(n, inputs, gates, cotangent, first_factor, second_factor, channel_gain):
    block, channels = inputs.shape
    jpd, nb = second_factor.shape[0], second_factor.shape[1]
    side = 4
    s_lanes = jnp.transpose(second_factor, (2, 1, 0)).reshape(nb, nb * jpd)
    tokens = jax.ShapeDtypeStruct((block, channels), BF16)
    pieces = pltpu.VMEM((side, side, jpd, channels), BF16)
    planes = pltpu.VMEM((side, side, side, jpd, channels), BF16)
    small = pltpu.VMEM((side, nb, block), BF16)
    dma = pltpu.SemaphoreType.DMA
    out, gin, ggate, gfirst, gsec, ggain = pl.pallas_call(
        functools.partial(fused_kernel, n),
        out_shape=(
            tokens, tokens, tokens,
            jax.ShapeDtypeStruct((block, block), BF16),
            jax.ShapeDtypeStruct((nb, block), BF16),
            jax.ShapeDtypeStruct((1, channels), F32),
        ),
        in_specs=[pl.BlockSpec(memory_space=pltpu.HBM)] * 4 + [pl.BlockSpec(memory_space=pltpu.VMEM)] * 2,
        out_specs=[pl.BlockSpec(memory_space=pltpu.VMEM)] * 6,
        scratch_shapes=[
            *[pltpu.VMEM((block, channels), BF16)] * 3,
            pltpu.VMEM((block, block), BF16),
            pltpu.VMEM((block, channels), F32),
            pltpu.VMEM((block, block), BF16),
            pltpu.VMEM((side, block, block), BF16),
            small,
            pieces, pieces, planes, planes, pieces, pieces, pieces, pieces, pieces, pieces,
            small, small,
            pltpu.VMEM((8, channels), F32),
            pltpu.VMEM((n, 1, channels), F32),
            dma((4, side, side)), dma((4, side, side)),
            dma((2, side, side)), dma((2, side, side)),
            dma((side,)), dma((side,)),
            dma((2, side)), dma((2, side)),
            dma((n,)), dma((n,)), dma((4,)),
        ],
        compiler_params=pltpu.CompilerParams(
            collective_id=0, has_side_effects=True, vmem_limit_bytes=48 * 1024 * 1024
        ),
    )(inputs, gates, cotangent, first_factor[0], s_lanes, channel_gain[None])
    gsec = jnp.transpose(gsec.reshape(nb, nb, jpd), (2, 1, 0))
    return out, gin, ggate, gfirst[None], gsec, ggain[0]


def exchanged(inputs, gates, cotangent, first_factor, second_factor, channel_gain):
    block_count, block_size = first_factor.shape[:2]
    token_rows, channels = inputs.shape
    mask_first = lower_mask(block_size)
    mask_second = lower_mask(second_factor.shape[1])
    first_masked = jnp.where(mask_first[None], first_factor, jnp.zeros((), BF16))
    second_masked = jnp.where(mask_second[None], second_factor, jnp.zeros((), BF16))
    norm_factor = 1.0 / math.sqrt(token_rows * lax.axis_size("seq"))
    by_block = lambda value: value.reshape(block_count, block_size, channels)
    rows3 = by_block(inputs)
    gates3 = by_block(gates).astype(F32)
    upstream3 = by_block(cotangent).astype(F32)
    to_cols = lambda value: lax.all_to_all(value, "seq", split_axis=1, concat_axis=0, tiled=True)
    to_rows = lambda value: lax.all_to_all(value, "seq", split_axis=0, concat_axis=1, tiled=True)
    product = functools.partial(jnp.einsum, preferred_element_type=F32)
    hidden_cols = to_cols((upstream3 * gates3 * channel_gain).astype(BF16))
    columns = to_cols(product("kab,kbc->kac", first_masked, rows3).astype(BF16))
    back_rows = to_rows(product("jab,ajc->bjc", second_masked, hidden_cols).astype(BF16))
    second_rows = to_rows(product("jab,bjc->ajc", second_masked, columns).astype(BF16)).astype(F32)
    pairs = product("ajc,bjc->jab", hidden_cols, columns)
    grad_sec = jnp.where(mask_second[None], pairs, 0.0).astype(BF16)
    pairs_first = product("kac,kbc->kab", back_rows, rows3)
    grad_first = jnp.where(mask_first[None], pairs_first, 0.0).astype(BF16)
    grad_in = product("kab,kac->kbc", first_masked, back_rows).astype(BF16)
    out = (gates3 * channel_gain * second_rows).astype(BF16)
    grad_gate = (upstream3 * channel_gain * second_rows).astype(BF16)
    gain_grad = lax.psum(jnp.sum(upstream3 * gates3 * second_rows, axis=(0, 1)), "seq") * norm_factor
    flat = lambda value: value.reshape(token_rows, channels)
    return flat(out), flat(grad_in), flat(grad_gate), grad_first, grad_sec, gain_grad


def on_device(*args):
    n = lax.axis_size("seq")
    first_factor, second_factor = args[3], args[4]
    if n == 16 and first_factor.shape[0] == 1 and second_factor.shape[0] % 16 == 0:
        return fused(n, *args)
    return exchanged(*args)


def solution(mesh):
    placed = (
        P(("groups", "seq"), None),
        P(("groups", "seq"), None),
        P(("groups", "seq"), None),
        P("seq", None, None),
        P("seq", None, None),
        P(),
    )
    return jax.shard_map(
        on_device,
        mesh=mesh,
        in_specs=placed,
        out_specs=(
            P(("groups", "seq"), None),
            P(("groups", "seq"), None),
            P(("groups", "seq"), None),
            P(("groups", "seq"), None, None),
            P(("groups", "seq"), None, None),
            P("groups"),
        ),
        check_vma=False,
    )
```
